512 devices in a mesh: req: 16 (over x, y), tp: 32 (over z, core).
Axes of the slice: x: 4, y: 4, z: 16, core: 2. Of those that a mesh axis runs over, the one named last changes fastest.
Arguments:
- tokens: bfloat16 [512, 16384], P(('req', 'tp')), may hold values from -6 to 6
- weight_codes: bfloat16 [16384, 53248], P('req', 'tp'), may hold values from -8 to 7, as said below
- weight_scales: bfloat16 [128, 53248], P('req', 'tp'), may hold values from 0.00077819824 to 0.003112793
- adapter_down: bfloat16 [64, 16384, 64], P('req', 'tp'), may hold values from -0.046875 to 0.046875
- adapter_up: bfloat16 [64, 64, 53248], P('req', None, 'tp'), may hold values from -0.375 to 0.375
- row_adapter: int32 [512], replicated, may hold values from 0 to 63, as said below
- adapter_slot: int32 [64], replicated, may hold values from 0 to 63, as said below
- live_rows: int32 [16], replicated, may hold values from 8 to 32, as said below
Outputs:
- projected: bfloat16 [512, 53248], P('req', 'tp')
The draws below stay inside these ranges and needn't reach their ends.
Inputs may be any that keep to these rules, and one draw needn't show every extreme that they name: `row_adapter`: the rows of one group name at most one adapter homed on each req device (adapter a is homed on req device adapter_slot[a] // 4); in every draw some group names an adapter of every req device, and every adapter is named. A permutation: adapter a lies at index adapter_slot[a] of the first dimension of adapter_down and adapter_up. `live_rows`: rows of a group at positions at or past its count are padding; some group is full. `weight_codes`: Integers.
All inputs are finite; a program needn't handle non-finite values.
Results may differ from the reference program's by a relative error of at most 0.015.
Values may be sent and summed in bfloat16 or wider, within the bound.
A program may use at most 64 MiB of HBM per device.

```python
import math
import jax
import jax.numpy as jnp
from jax import lax

D = 16384
FF = 53248
RANK = 64
QGROUP = 128
GROUP_ROWS = 32
ADAPT_DEV = 4
ROWS = 512
ADAPTERS = 64
N_REQ = 16


def routing_tables(key):
    key_list = jax.random.split(key, 8)
    adapter_order = jax.random.permutation(key_list[0], ADAPTERS).astype(jnp.int32)
    owners = jnp.argsort(adapter_order, stable=True).astype(jnp.int32)
    group_axis = jnp.arange(N_REQ, dtype=jnp.int32)
    rotation = jax.random.randint(key_list[1], (), 0, N_REQ)
    turned = (group_axis + rotation) % N_REQ
    offsets = jax.random.randint(key_list[2], (N_REQ,), 0, ADAPT_DEV)
    forced = turned[:, None] < ADAPT_DEV
    picked = jnp.where(forced, (turned[:, None] + offsets[None, :]) % ADAPT_DEV, jax.random.randint(key_list[3], (N_REQ, N_REQ), 0, ADAPT_DEV))
    first_home = jax.random.randint(key_list[4], (N_REQ, 1), 0, N_REQ)
    in_use = jnp.where(forced | (group_axis[None, :] == first_home), 1, jax.random.randint(key_list[5], (N_REQ, N_REQ), 0, 2))
    ranking = jax.random.randint(key_list[6], (N_REQ, N_REQ), 0, 1 << 20) * N_REQ + group_axis[None, :] + 1
    ordered = jnp.argsort(-(in_use * ranking), axis=1, stable=True).astype(jnp.int32)
    used_count = jnp.sum(in_use, axis=1, keepdims=True)
    row_keys = jax.random.split(key_list[7], 3)
    shuffle = jax.random.randint(row_keys[0], (N_REQ, GROUP_ROWS), 0, 1 << 20) * GROUP_ROWS + jnp.arange(GROUP_ROWS, dtype=jnp.int32)[None, :]
    position = jnp.argsort(jnp.argsort(shuffle, axis=1, stable=True), axis=1, stable=True).astype(jnp.int32)
    first_draw = jax.random.randint(row_keys[1], (N_REQ, GROUP_ROWS), 0, used_count)
    second_draw = jax.random.randint(row_keys[2], (N_REQ, GROUP_ROWS), 0, used_count)
    choose = jnp.where(position < used_count, position, jnp.minimum(first_draw, second_draw))
    home_of_row = jnp.take_along_axis(ordered, choose, axis=1)
    local_of_row = jnp.take_along_axis(picked, home_of_row, axis=1)
    assigned = owners[home_of_row * ADAPT_DEV + local_of_row].reshape(ROWS)
    return (adapter_order, assigned.astype(jnp.int32))


def draw_adapter_slot(key, part):
    adapter_order, assigned = routing_tables(key)
    return adapter_order


def draw_row_adapter(key, part):
    adapter_order, assigned = routing_tables(key)
    return assigned


def draw_live_rows(key, part):
    key = jax.random.fold_in(key, 9)
    key_list = jax.random.split(key, 3)
    counts_drawn = jax.random.randint(key_list[0], (N_REQ,), GROUP_ROWS // 4, GROUP_ROWS + 1)
    full_group = jax.random.randint(key_list[1], (), 0, N_REQ)
    short_group = (full_group + 1 + jax.random.randint(key_list[2], (), 0, N_REQ - 1)) % N_REQ
    group_axis = jnp.arange(N_REQ, dtype=jnp.int32)
    counts_drawn = jnp.where(group_axis == short_group, GROUP_ROWS // 4, counts_drawn)
    counts_drawn = jnp.where(group_axis == full_group, GROUP_ROWS, counts_drawn)
    return counts_drawn.astype(jnp.int32)


def draw_weight_codes(key, part):
    key = jax.random.fold_in(key, 5)
    values = jax.random.randint(key, (D, FF), -8, 8)
    return values.astype(jnp.float32).astype(jnp.bfloat16)


def block_levels(key, dims, cuts, low, high):
    def one(dim, blocks):
        heights = jax.random.uniform(jax.random.fold_in(jax.random.fold_in(key, 6), dim), (blocks,), jnp.float32, low / len(cuts), high / len(cuts))
        return jnp.repeat(jnp.exp(heights), dims[dim] // blocks).reshape((-1,) + (1,) * (len(dims) - dim - 1))

    level = one(*cuts[0])
    for cut in cuts[1:]:
        level = level * one(*cut)
    return level


def bell_draw(stream_key, dims, scale, most, cuts=(), kind=jnp.bfloat16):
    result = scale * jax.random.normal(stream_key, dims, jnp.float32)
    if cuts:
        result = result * block_levels(stream_key, dims, cuts, -0.22, 0.18)
    return jnp.clip(result, -most, most).astype(kind)


def setup_inputs(seed: int = 0) -> dict:
    splits = jax.random.split(jax.random.key(seed), 9)
    return {
        "tokens": bell_draw(splits[0], (ROWS, D), 1.0, 6.0, ((0, 512),)),
        "weight_codes": draw_weight_codes(jax.random.fold_in(splits[8], 71), 0),
        "weight_scales": jnp.clip(jnp.exp(math.log(0.003112793) - 1.3862944 * jax.random.uniform(splits[2], (D // QGROUP, FF), jnp.float32) ** block_levels(splits[2], (D // QGROUP, FF), ((0, 16), (1, 32)), -0.2, 0.2)), 0.00077819824, 0.003112793).astype(jnp.bfloat16),
        "adapter_down": bell_draw(splits[3], (ADAPTERS, D, RANK), D ** -0.5, 0.046875, ((0, 16), (1, 32))),
        "adapter_up": bell_draw(splits[4], (ADAPTERS, RANK, FF), (4 * RANK) ** -0.5, 0.375, ((0, 16), (2, 32))),
        "row_adapter": draw_row_adapter(jax.random.fold_in(splits[8], 71), 0),
        "adapter_slot": draw_adapter_slot(jax.random.fold_in(splits[8], 71), 0),
        "live_rows": draw_live_rows(jax.random.fold_in(splits[8], 71), 0),
    }


adapter_scale = 2.0


def reference(tokens, weight_codes, weight_scales, adapter_down, adapter_up, row_adapter, adapter_slot, live_rows):
    block_width = D // N_REQ
    code_blocks = weight_codes.reshape(N_REQ, block_width, FF)
    scale_blocks = weight_scales.reshape(N_REQ, block_width // QGROUP, FF)
    token_blocks = tokens.reshape(ROWS, N_REQ, block_width).transpose(1, 0, 2)

    def add_block(carry, pieces):
        codes_piece, scales_piece, token_piece = pieces
        weight = (codes_piece.reshape(block_width // QGROUP, QGROUP, FF).astype(jnp.float32)
                  * scales_piece.astype(jnp.float32)[:, None, :]).reshape(block_width, FF).astype(jnp.bfloat16)
        product = jnp.dot(token_piece, weight, preferred_element_type=jnp.float32)
        rounded = lax.optimization_barrier(product.astype(jnp.bfloat16)).astype(jnp.float32)
        return carry + rounded, None

    base_sum, _ = lax.scan(add_block, jnp.zeros((ROWS, FF), jnp.float32), (code_blocks, scale_blocks, token_blocks))

    row_slots = adapter_slot[row_adapter].astype(jnp.int32)
    row_block = math.gcd(ROWS, 16)

    def adapter_rows(pieces):
        token_piece, slot_piece = pieces
        down_rows = adapter_down[slot_piece].astype(jnp.float32)
        reduced = jnp.einsum('bd,bdr->br', token_piece.astype(jnp.float32), down_rows, precision=lax.Precision.HIGHEST)
        reduced = lax.optimization_barrier(reduced.astype(jnp.bfloat16)).astype(jnp.float32)
        up_rows = adapter_up[slot_piece].astype(jnp.float32)
        return jnp.einsum('br,brf->bf', reduced, up_rows, precision=lax.Precision.HIGHEST)

    adapter_term = lax.map(adapter_rows, (tokens.reshape(ROWS // row_block, row_block, D),
                                          row_slots.reshape(ROWS // row_block, row_block))).reshape(ROWS, FF)
    row_numbers = jnp.arange(ROWS, dtype=jnp.int32)
    live_mask = (row_numbers % GROUP_ROWS) < live_rows[row_numbers // GROUP_ROWS]
    return jnp.where(live_mask[:, None], base_sum + adapter_scale * adapter_term, 0.0).astype(jnp.bfloat16)
```

```python
import functools

import jax
import jax.numpy as jnp
from jax import lax
from jax.experimental import pallas as pl
from jax.experimental.pallas import tpu as pltpu
from jax.sharding import PartitionSpec as P

MESH = pl.DeviceIdType.MESH
F32 = jnp.float32
BF16 = jnp.bfloat16
LANES = 128
SIDE = 4
HOMES = SIDE * SIDE
LAYERS = 16
HALF = HOMES // 2
adapter_scale = 2.0


def iota(shape, axis):
    return lax.broadcasted_iota(jnp.int32, shape, axis)


def ones_where(mask, dtype=BF16):
    return jnp.where(mask, 1.0, 0.0).astype(dtype)


def dot(a, b):
    return jnp.dot(a, b, preferred_element_type=F32)


def kernel(
    tok_hbm,
    codes_hbm,
    scales_hbm,
    down_hbm,
    up_hbm,
    row_ref,
    slot_ref,
    live_ref,
    out_ref,
    tok,
    codes,
    scales,
    down,
    up,
    mine,
    other,
    pairs,
    tiles,
    feats,
    onehot,
    wanted,
    packed,
    send_down,
    got_down,
    weight,
    shuffle,
    lhs,
    low_lhs,
    select,
    low_send,
    low_got,
    low_sum,
    low_sib,
    red_send,
    red,
    expand,
    spread,
    mask,
    total,
    part,
    got_part,
    half_sum,
    got_half,
    load_sem,
    sib_s,
    sib_r,
    blk_s,
    blk_r,
    slc_s,
    slc_r,
    dwn_s,
    dwn_r,
    zg1_s,
    zg1_r,
    zg2_s,
    zg2_r,
    zg3_s,
    zg3_r,
    low_s,
    low_r,
    red_s,
    red_r,
    rs1_s,
    rs1_r,
    rs2_s,
    rs2_r,
):
    g = lax.axis_index("req")
    t = lax.axis_index("tp")
    x, y = g // SIDE, g % SIDE
    z, c = t // 2, t % 2
    sib = (g, z * 2 + 1 - c)
    chunks = weight.shape[0]
    depth = weight.shape[1]
    groups = depth // LANES
    rank = down.shape[2]
    per_home = down.shape[0]
    adapters = HOMES * per_home
    group_rows = 2 * LAYERS
    lane_width = down.shape[1]
    half_width = lane_width // 2

    def plane(i):
        return lax.rem(x + i // SIDE, SIDE) * SIDE + lax.rem(y + i % SIDE, SIDE)

    def plane_from(i):
        return lax.rem(x + SIDE - i // SIDE, SIDE) * SIDE + lax.rem(y + SIDE - i % SIDE, SIDE)

    def layer(i):
        return lax.rem(z + i + LAYERS, LAYERS)

    def rcopy(src, dst, ss, rs, dev):
        return pltpu.make_async_remote_copy(
            src_ref=src, dst_ref=dst, send_sem=ss, recv_sem=rs, device_id=dev, device_id_type=MESH
        )

    def each(lo, hi, fn):
        def step(i, carry):
            fn(i)
            return carry

        lax.fori_loop(lo, hi, step, 0)

    barrier = pltpu.get_barrier_semaphore()

    def greet(i):
        pl.semaphore_signal(barrier, inc=1, device_id=(plane(i), t), device_id_type=MESH)
        pl.semaphore_signal(barrier, inc=1, device_id=(g, layer(i) * 2 + c), device_id_type=MESH)

    pl.semaphore_signal(barrier, inc=1, device_id=sib, device_id_type=MESH)
    each(1, HOMES, greet)

    loads = [
        pltpu.make_async_copy(src, dst, load_sem.at[i])
        for i, (src, dst) in enumerate(
            [(tok_hbm, tok), (down_hbm, down), (codes_hbm, codes), (scales_hbm, scales), (up_hbm, up)]
        )
    ]
    for load in loads:
        load.start()

    rows = row_ref[...]
    slots = jnp.zeros_like(rows)
    for a in range(adapters):
        slots = jnp.where(rows == a, slot_ref[a], slots)
    eye = ones_where(iota((adapters, adapters), 0) == iota((adapters, adapters), 1))
    for b in range(rows.shape[0]):
        hit = ones_where(slots[b : b + 1, :] == iota((adapters, LANES), 0))
        onehot[b * LANES : (b + 1) * LANES, :] = lax.dot_general(
            hit, eye, (((0,), (0,)), ((), ())), preferred_element_type=F32
        )
    all_rows = onehot.shape[0]
    in_group = ones_where(iota((HOMES, all_rows), 1) // group_rows == iota((HOMES, all_rows), 0))
    named = dot(in_group, onehot[...].astype(BF16))
    pick = ones_where(
        iota((adapters, per_home * LANES), 0) == g * per_home + iota((adapters, per_home * LANES), 1) // LANES
    )
    wanted[...] = jnp.where(dot(named.astype(BF16), pick) > 0, 1.0, 0.0)

    loads[0].wait()
    row = tok[...].astype(F32)
    for b in range(mine.shape[0] // 16):
        mine[b * 16 : (b + 1) * 16, :] = jnp.concatenate(
            [row[:, (b * 16 + i) * LANES : (b * 16 + i + 1) * LANES] for i in range(16)], axis=0
        ).astype(BF16)

    loads[1].wait()
    to_low = ones_where(iota((rank, LANES), 0) == iota((rank, LANES), 1))
    to_high = ones_where(iota((rank, LANES), 0) + rank == iota((rank, LANES), 1))
    for a in range(per_home):
        packed[a] = dot(down[a, :half_width, :], to_low) + dot(down[a, half_width:, :], to_high)

    def choose(b):
        weights = wanted[pl.ds(b, 1), :]
        block = packed[0] * weights[:, :LANES]
        for a in range(1, per_home):
            block += packed[a] * weights[:, a * LANES : (a + 1) * LANES]
        send_down[b] = block.astype(BF16)

    each(0, HOMES, choose)

    pl.semaphore_wait(barrier, 2 * (HOMES - 1) + 1)

    swap = rcopy(mine, other, sib_s.at[0], sib_r.at[0], sib)
    swap.start()
    swap.wait_recv()
    for b in range(HOMES // 2):
        own = mine[b * 16 : (b + 1) * 16, :].astype(F32)
        theirs = other[b * 16 : (b + 1) * 16, :].astype(F32)
        first = jnp.where(c == 0, own, theirs)
        second = jnp.where(c == 0, theirs, own)
        pairs[2 * b] = jnp.concatenate([first[:8], second[:8]], axis=0).astype(BF16)
        pairs[2 * b + 1] = jnp.concatenate([first[8:], second[8:]], axis=0).astype(BF16)

    carrier = g // HALF == c

    def block_copy(i):
        b = plane(i)
        return rcopy(pairs.at[b], tiles.at[c, z, g % HALF], blk_s.at[i], blk_r.at[i], (b, t))

    def slice_copy(i):
        d = layer(i)
        return rcopy(pairs.at[d], feats.at[z], slc_s.at[i], slc_r.at[i], (g, d * 2 + c))

    def down_copy(i):
        b = plane(i)
        return rcopy(send_down.at[b], got_down.at[g], dwn_s.at[i], dwn_r.at[i], (b, t))

    @pl.when(carrier)
    def _():
        each(1, HOMES, lambda i: block_copy(i).start())
        tiles[c, z, g % HALF] = pairs[g]

    each(1, LAYERS, lambda i: slice_copy(i).start())
    feats[z] = pairs[z]
    each(1, HOMES, lambda i: down_copy(i).start())
    got_down[g] = send_down[g]

    by_home = ones_where(iota((adapters, HOMES * LANES), 0) // per_home == iota((adapters, HOMES * LANES), 1) // LANES)
    select[...] = dot(onehot[pl.ds(pl.multiple_of(g * group_rows, group_rows), group_rows), :].astype(BF16), by_home)

    def place(b):
        return jnp.where(c == 0, b, (b % SIDE) * SIDE + b // SIDE)

    own_lanes = ones_where(
        iota((adapters, per_home * rank), 0) == g * per_home + iota((adapters, per_home * rank), 1) // rank
    )

    def own_mask(b):
        mask[pl.ds(pl.multiple_of(place(b) * group_rows, group_rows), group_rows), :] = dot(
            onehot[pl.ds(pl.multiple_of(b * group_rows, group_rows), group_rows), :].astype(BF16), own_lanes
        )

    loads[2].wait()
    loads[3].wait()

    def dequantize(k):
        cols = pl.ds(pl.multiple_of(k * LANES, LANES), LANES)
        scale = scales[:, cols].astype(F32)
        for j in range(groups):
            weight[k, j * LANES : (j + 1) * LANES, :] = (
                codes[j * LANES : (j + 1) * LANES, cols].astype(F32) * scale[j : j + 1, :]
            ).astype(BF16)

    each(0, chunks // 2, dequantize)

    def wait_block(i):
        @pl.when(plane_from(i) // HALF == c)
        def _():
            block_copy(i).wait_recv()

    each(1, HOMES, wait_block)

    far = (3, -3, 6, -6)

    def far_copy(n):
        return rcopy(
            tiles.at[c, z], tiles.at[c, z], zg1_s.at[n], zg1_r.at[n], (g, layer(far[n]) * 2 + c)
        )

    near = [(src, step) for src in (0, -3, 3, -6, 6) for step in (1, -1)]

    def near_copy(n):
        src, step = near[n]
        s = layer(src)
        return rcopy(tiles.at[c, s], tiles.at[c, s], zg2_s.at[n], zg2_r.at[n], (g, layer(step) * 2 + c))

    quarter = HALF // 2

    def last_copy(n):
        src, step = ((-6, 2), (6, -2))[n]
        s = layer(src)
        some = tiles.at[c, s, pl.ds(n * quarter, quarter)]
        return rcopy(some, some, zg3_s.at[n], zg3_r.at[n], (g, layer(step) * 2 + c))

    for n in range(4):
        far_copy(n).start()
    for n in range(2):
        near_copy(n).start()

    each(chunks // 2, chunks, dequantize)
    each(0, HOMES, own_mask)

    each(1, LAYERS, lambda i: slice_copy(i).wait_recv())
    shuffle[...] = feats[...].astype(F32).reshape(LAYERS * 16, LANES)
    for j in range(lane_width // LANES):
        low_lhs[:, j * LANES : (j + 1) * LANES] = shuffle[
            pl.ds(c * (lane_width // LANES) + j, group_rows, stride=8), :
        ].astype(BF16)

    each(1, HOMES, lambda i: down_copy(i).wait_recv())
    first = jnp.zeros((group_rows, LANES), F32)
    second = jnp.zeros((group_rows, LANES), F32)
    for b in range(HOMES):
        here = select[:, b * LANES : (b + 1) * LANES]
        first += here * dot(low_lhs[:, :half_width], got_down[b])
        second += here * dot(low_lhs[:, half_width:], got_down[b])
    reduced = first + pltpu.roll(second, rank, 1)
    low = jnp.where(
        iota((LAYERS, LANES), 1) < rank, reduced[:LAYERS], pltpu.roll(reduced[LAYERS:], rank, 1)
    )
    low_sum[...] = low
    low_send[...] = low.astype(BF16)

    def low_copy(i):
        return rcopy(low_send, low_got.at[z], low_s.at[i], low_r.at[i], (g, layer(i) * 2 + c))

    each(1, LAYERS, lambda i: low_copy(i).start())

    for n, come in enumerate((-3, 3, -6, 6)):
        far_copy(n).wait_recv()
        near_copy(2 + 2 * n).start()
        near_copy(3 + 2 * n).start()
    last_copy(0).start()
    last_copy(1).start()

    low_got[z] = jnp.zeros((LAYERS, LANES), BF16)
    each(1, LAYERS, lambda i: low_copy(i).wait_recv())
    acc = low_sum[...]
    for b in range(LAYERS):
        acc += low_got[b].astype(F32)
    low_sum[...] = acc
    swap_low = rcopy(low_sum, low_sib, sib_s.at[1], sib_r.at[1], sib)
    swap_low.start()
    swap_low.wait_recv()
    red_send[...] = (low_sum[...] + low_sib[...]).astype(BF16)

    def red_copy(i):
        return rcopy(red_send, red.at[g], red_s.at[i], red_r.at[i], (plane(i), t))

    each(1, HOMES, lambda i: red_copy(i).start())
    red[g] = red_send[...]

    for n in range(len(near)):
        near_copy(n).wait_recv()
    last_copy(0).wait_recv()
    last_copy(1).wait_recv()
    swap_tiles = rcopy(tiles.at[c], tiles.at[c], sib_s.at[2], sib_r.at[2], sib)
    swap_tiles.start()
    swap_tiles.wait_recv()

    def arrange(b):
        shuffle[...] = tiles[b // HALF, :, b % HALF].astype(F32).reshape(LAYERS * 16, LANES)
        here = pl.ds(pl.multiple_of(place(b) * group_rows, group_rows), group_rows)
        for j in range(groups):
            lhs[here, j * LANES : (j + 1) * LANES] = shuffle[pl.ds(j, group_rows, stride=8), :].astype(BF16)

    each(0, HOMES, arrange)

    def base(k):
        total[k] = dot(lhs[...], weight[k])

    each(0, chunks, base)

    each(1, HOMES, lambda i: red_copy(i).wait_recv())
    spread_from = iota((LANES, 2 * per_home * rank), 0)
    spread_to = iota((LANES, 2 * per_home * rank), 1)
    copies = ones_where(
        spread_from == spread_to % rank + (spread_to // (per_home * rank)) * rank
    )
    wide = per_home * rank
    expand[...] = dot(red[...].reshape(HOMES * LAYERS, LANES), copies)
    for b in range(HOMES):
        here = pl.multiple_of(place(b) * group_rows, group_rows)
        lines = expand[b * LAYERS : (b + 1) * LAYERS, :]
        top = pl.ds(here, LAYERS)
        bottom = pl.ds(pl.multiple_of(here + LAYERS, LAYERS), LAYERS)
        spread[top, :] = (lines[:, :wide] * mask[top, :]).astype(BF16)
        spread[bottom, :] = (lines[:, wide:] * mask[bottom, :]).astype(BF16)

    loads[4].wait()
    first_at = jnp.where(c == 0, x, y)
    second_at = jnp.where(c == 0, y, x)
    four = SIDE * group_rows

    def along_first(d):
        to = lax.rem(first_at + d, SIDE)
        return to, (jnp.where(c == 0, to * SIDE + y, x * SIDE + to), t)

    def along_second(d):
        to = lax.rem(second_at + d, SIDE)
        return to, (jnp.where(c == 0, x * SIDE + to, to * SIDE + y), t)

    def part_copy(k, d):
        to, dev = along_first(d)
        src = part.at[k, pl.ds(pl.multiple_of(to * four, four), four)]
        return rcopy(src, got_part.at[k, d - 1], rs1_s.at[k, d - 1], rs1_r.at[k, d - 1], dev)

    def half_copy(k, d):
        to, dev = along_second(d)
        src = half_sum.at[k, pl.ds(pl.multiple_of(to * group_rows, group_rows), group_rows)]
        return rcopy(src, got_half.at[k, d - 1], rs2_s.at[k, d - 1], rs2_r.at[k, d - 1], dev)

    def send_part(k):
        cols = pl.ds(pl.multiple_of(k * LANES, LANES), LANES)
        part[k] = (total[k] + adapter_scale * dot(spread[...], up[:, cols])).astype(BF16)
        for d in range(1, SIDE):
            part_copy(k, d).start()

    each(0, chunks, send_part)

    def send_half(k):
        own = part[k, pl.ds(pl.multiple_of(first_at * four, four), four), :].astype(F32)
        for d in range(1, SIDE):
            part_copy(k, d).wait_recv()
            own += got_part[k, d - 1].astype(F32)
        half_sum[k] = own.astype(BF16)
        for d in range(1, SIDE):
            half_copy(k, d).start()

    each(0, chunks, send_half)

    live = iota((group_rows, LANES), 0) < live_ref[g]

    def finish(k):
        own = half_sum[k, pl.ds(pl.multiple_of(second_at * group_rows, group_rows), group_rows), :].astype(F32)
        for d in range(1, SIDE):
            half_copy(k, d).wait_recv()
            own += got_half[k, d - 1].astype(F32)
        out_ref[:, pl.ds(pl.multiple_of(k * LANES, LANES), LANES)] = jnp.where(live, own, 0.0).astype(BF16)

    each(0, chunks, finish)

    swap.wait_send()
    swap_low.wait_send()
    swap_tiles.wait_send()

    @pl.when(carrier)
    def _():
        each(1, HOMES, lambda i: block_copy(i).wait_send())

    def sent(i):
        slice_copy(i).wait_send()
        down_copy(i).wait_send()
        low_copy(i).wait_send()
        red_copy(i).wait_send()

    each(1, HOMES, sent)
    for n in range(4):
        far_copy(n).wait_send()
    for n in range(len(near)):
        near_copy(n).wait_send()
    last_copy(0).wait_send()
    last_copy(1).wait_send()

    def sent_parts(k):
        for d in range(1, SIDE):
            part_copy(k, d).wait_send()
            half_copy(k, d).wait_send()

    each(0, chunks, sent_parts)


def body(tokens, weight_codes, weight_scales, adapter_down, adapter_up, row_adapter, adapter_slot, live_rows):
    width = tokens.shape[1]
    depth, columns = weight_codes.shape
    per_home, lane_width, rank = adapter_down.shape
    all_rows = row_adapter.shape[0]
    group_rows = all_rows // HOMES
    chunks = columns // LANES
    wide = per_home * rank
    up = adapter_up.reshape(wide, columns)
    rows = row_adapter.reshape(all_rows // LANES, LANES)
    vmem, dma = pltpu.VMEM, pltpu.SemaphoreType.DMA
    scratch = [
        vmem((1, width), BF16),
        vmem((depth, columns), BF16),
        vmem(weight_scales.shape, BF16),
        vmem(adapter_down.shape, BF16),
        vmem((wide, columns), BF16),
        vmem((width // LANES, LANES), BF16),
        vmem((width // LANES, LANES), BF16),
        vmem((HOMES, 16, LANES), BF16),
        vmem((2, LAYERS, HALF, 16, LANES), BF16),
        vmem((LAYERS, 16, LANES), BF16),
        vmem((all_rows, HOMES * per_home), F32),
        vmem((HOMES, per_home * LANES), F32),
        vmem((per_home, lane_width // 2, LANES), F32),
        vmem((HOMES, lane_width // 2, LANES), BF16),
        vmem((HOMES, lane_width // 2, LANES), BF16),
        vmem((chunks, depth, LANES), BF16),
        vmem((LAYERS * 16, LANES), F32),
        vmem((all_rows, depth), BF16),
        vmem((group_rows, lane_width), BF16),
        vmem((group_rows, HOMES * LANES), F32),
        vmem((LAYERS, LANES), BF16),
        vmem((LAYERS, LAYERS, LANES), BF16),
        vmem((LAYERS, LANES), F32),
        vmem((LAYERS, LANES), F32),
        vmem((LAYERS, LANES), BF16),
        vmem((HOMES, LAYERS, LANES), BF16),
        vmem((HOMES * LAYERS, 2 * wide), F32),
        vmem((all_rows, wide), BF16),
        vmem((all_rows, wide), F32),
        vmem((chunks, all_rows, LANES), F32),
        vmem((chunks, all_rows, LANES), BF16),
        vmem((chunks, SIDE - 1, SIDE * group_rows, LANES), BF16),
        vmem((chunks, SIDE * group_rows, LANES), BF16),
        vmem((chunks, SIDE - 1, group_rows, LANES), BF16),
        dma((5,)),
        dma((3,)),
        dma((3,)),
    ]
    for count in (HOMES, LAYERS, HOMES, 4, 10, 2, LAYERS, HOMES):
        scratch += [dma((count,)), dma((count,))]
    scratch += [dma((chunks, SIDE - 1))] * 4
    return pl.pallas_call(
        kernel,
        out_shape=jax.ShapeDtypeStruct((group_rows, columns), BF16),
        in_specs=[pl.BlockSpec(memory_space=pl.ANY)] * 5
        + [pl.BlockSpec(memory_space=pltpu.VMEM)]
        + [pl.BlockSpec(memory_space=pltpu.SMEM)] * 2,
        out_specs=pl.BlockSpec(memory_space=pltpu.VMEM),
        scratch_shapes=scratch,
        compiler_params=pltpu.CompilerParams(
            collective_id=0, has_side_effects=True, vmem_limit_bytes=48 * 1024 * 1024
        ),
    )(tokens, weight_codes, weight_scales, adapter_down, up, rows, adapter_slot, live_rows)


def solution(mesh):
    in_specs = (
        P(("req", "tp"), None),
        P("req", "tp"),
        P("req", "tp"),
        P("req", "tp", None),
        P("req", None, "tp"),
        P(),
        P(),
        P(),
    )
    return jax.shard_map(body, mesh=mesh, in_specs=in_specs, out_specs=P("req", "tp"), check_vma=False)
```

```python
import functools

import jax
import jax.numpy as jnp
from jax import lax
from jax.experimental import pallas as pl
from jax.experimental.pallas import tpu as pltpu
from jax.sharding import PartitionSpec as P

MESH = pl.DeviceIdType.MESH
F32 = jnp.float32
BF16 = jnp.bfloat16
LANES = 128
SIDE = 4
HOMES = SIDE * SIDE
LAYERS = 16
HALF = HOMES // 2
adapter_scale = 2.0


def iota(shape, axis):
    return lax.broadcasted_iota(jnp.int32, shape, axis)


def ones_where(mask, dtype=BF16):
    return jnp.where(mask, 1.0, 0.0).astype(dtype)


def dot(a, b):
    return jnp.dot(a, b, preferred_element_type=F32)


def kernel(
    tok_hbm,
    codes_hbm,
    scales_hbm,
    down_hbm,
    up_hbm,
    row_hbm,
    slot_hbm,
    live_hbm,
    out_ref,
    row_ref,
    slot_ref,
    live_ref,
    tok,
    codes,
    scales,
    down,
    up,
    mine,
    other,
    pairs,
    tiles,
    feats,
    onehot,
    wanted,
    send_down,
    got_down,
    weight,
    shuffle,
    lhs,
    low_lhs,
    select,
    low_send,
    low_got,
    low_sum,
    low_sib,
    red_send,
    red,
    expand,
    spread,
    mask,
    total,
    part,
    got_part,
    half_sum,
    got_half,
    load_sem,
    sib_s,
    sib_r,
    blk_s,
    blk_r,
    slc_s,
    slc_r,
    dwn_s,
    dwn_r,
    zg1_s,
    zg1_r,
    zg2_s,
    zg2_r,
    zg3_s,
    zg3_r,
    pas_s,
    pas_r,
    low_s,
    low_r,
    red_s,
    red_r,
    rs1_s,
    rs1_r,
    rs2_s,
    rs2_r,
):
    g = lax.axis_index("req")
    t = lax.axis_index("tp")
    x, y = g // SIDE, g % SIDE
    z, c = t // 2, t % 2
    sib = (g, z * 2 + 1 - c)
    depth, columns = weight.shape
    chunks = columns // LANES
    groups = depth // LANES
    per_home, rank, lane_width = down.shape
    adapters = HOMES * per_home
    group_rows = 2 * LAYERS

    def plane(i):
        return lax.rem(x + i // SIDE, SIDE) * SIDE + lax.rem(y + i % SIDE, SIDE)

    def plane_from(i):
        return lax.rem(x + SIDE - i // SIDE, SIDE) * SIDE + lax.rem(y + SIDE - i % SIDE, SIDE)

    def layer(i):
        return lax.rem(z + i + LAYERS, LAYERS)

    def rcopy(src, dst, ss, rs, dev):
        return pltpu.make_async_remote_copy(
            src_ref=src, dst_ref=dst, send_sem=ss, recv_sem=rs, device_id=dev, device_id_type=MESH
        )

    early = 4
    across = (10, 9, 11, 6, 14, 5, 7, 13, 15, 8, 2, 1, 3, 4, 12)
    along = (8, 7, 9, 6, 10, 5, 11, 4, 12, 3, 13, 2, 14, 1, 15)

    def in_order(order, fn):
        for i in order:
            fn(i)

    def each(lo, hi, fn):
        def step(i, carry):
            fn(i)
            return carry

        lax.fori_loop(lo, hi, step, 0)

    barrier = pltpu.get_barrier_semaphore()

    def greet(i):
        pl.semaphore_signal(barrier, inc=1, device_id=(plane(i), t), device_id_type=MESH)
        pl.semaphore_signal(barrier, inc=1, device_id=(g, layer(i) * 2 + c), device_id_type=MESH)

    pl.semaphore_signal(barrier, inc=1, device_id=sib, device_id_type=MESH)
    each(1, HOMES, greet)

    loads = [
        pltpu.make_async_copy(src, dst, load_sem.at[i])
        for i, (src, dst) in enumerate(
            [
                (tok_hbm, tok),
                (down_hbm, down),
                (codes_hbm, codes),
                (scales_hbm, scales),
                (up_hbm, up),
                (row_hbm, row_ref),
                (slot_hbm, slot_ref),
                (live_hbm, live_ref),
            ]
        )
    ]
    for i in (5, 6, 1, 0, 2, 3, 4, 7):
        loads[i].start()

    loads[0].wait()
    row = tok[...].astype(F32)
    for b in range(mine.shape[0] // 16):
        mine[b * 16 : (b + 1) * 16, :] = jnp.concatenate(
            [row[:, (b * 16 + i) * LANES : (b * 16 + i + 1) * LANES] for i in range(16)], axis=0
        ).astype(BF16)

    loads[5].wait()
    loads[6].wait()
    rows = row_ref[...]
    slots = jnp.zeros_like(rows)
    for a in range(adapters):
        slots = jnp.where(rows == a, slot_ref[a], slots)
    eye = ones_where(iota((adapters, adapters), 0) == iota((adapters, adapters), 1))
    for b in range(rows.shape[0]):
        hit = ones_where(slots[b : b + 1, :] == iota((adapters, LANES), 0))
        onehot[b * LANES : (b + 1) * LANES, :] = lax.dot_general(
            hit, eye, (((0,), (0,)), ((), ())), preferred_element_type=F32
        )
    all_rows = onehot.shape[0]
    in_group = ones_where(iota((HOMES, all_rows), 1) // group_rows == iota((HOMES, all_rows), 0))
    named = dot(in_group, onehot[...].astype(BF16))
    pick = ones_where(
        iota((adapters, per_home * lane_width), 0)
        == g * per_home + iota((adapters, per_home * lane_width), 1) // lane_width
    )
    wanted[...] = jnp.where(dot(named.astype(BF16), pick) > 0, 1.0, 0.0)

    loads[1].wait()

    def choose(b):
        line = wanted[pl.ds(b, 1), :]
        weights = [
            jnp.broadcast_to(line[:, a * lane_width : (a + 1) * lane_width], (16, lane_width)).astype(BF16)
            for a in range(per_home)
        ]
        for i in range(rank // 16):
            lines = slice(i * 16, (i + 1) * 16)
            block = down[0, lines, :] * weights[0]
            for a in range(1, per_home):
                block += down[a, lines, :] * weights[a]
            send_down[b, lines, :] = block

    each(0, HOMES, choose)

    pl.semaphore_wait(barrier, 2 * (HOMES - 1) + 1)

    def down_copy(i):
        b = plane(i)
        return rcopy(send_down.at[b], got_down.at[g], dwn_s.at[i], dwn_r.at[i], (b, t))

    swap = rcopy(mine, other, sib_s.at[0], sib_r.at[0], sib)
    swap.start()
    in_order(across[:early], lambda i: down_copy(i).start())
    swap.wait_recv()
    for b in range(HOMES // 2):
        own = mine[b * 16 : (b + 1) * 16, :].astype(F32)
        theirs = other[b * 16 : (b + 1) * 16, :].astype(F32)
        first = jnp.where(c == 0, own, theirs)
        second = jnp.where(c == 0, theirs, own)
        pairs[2 * b] = jnp.concatenate([first[:8], second[:8]], axis=0).astype(BF16)
        pairs[2 * b + 1] = jnp.concatenate([first[8:], second[8:]], axis=0).astype(BF16)

    carrier = g // HALF == c

    def block_copy(i):
        b = plane(i)
        return rcopy(pairs.at[b], tiles.at[c, z, g % HALF], blk_s.at[i], blk_r.at[i], (b, t))

    def slice_copy(i):
        d = layer(i)
        return rcopy(pairs.at[d], feats.at[z], slc_s.at[i], slc_r.at[i], (g, d * 2 + c))

    @pl.when(carrier)
    def _():
        in_order(across, lambda i: block_copy(i).start())
        tiles[c, z, g % HALF] = pairs[g]

    in_order(along, lambda i: slice_copy(i).start())
    feats[z] = pairs[z]
    in_order(across[early:], lambda i: down_copy(i).start())
    got_down[g] = send_down[g]

    by_home = ones_where(iota((adapters, HOMES * rank), 0) // per_home == iota((adapters, HOMES * rank), 1) // rank)
    select[...] = dot(onehot[pl.ds(pl.multiple_of(g * group_rows, group_rows), group_rows), :].astype(BF16), by_home)

    def place(b):
        return jnp.where(c == 0, b, (b % SIDE) * SIDE + b // SIDE)

    own_lanes = ones_where(
        iota((adapters, per_home * rank), 0) == g * per_home + iota((adapters, per_home * rank), 1) // rank
    )

    def own_mask(b):
        mask[pl.ds(pl.multiple_of(place(b) * group_rows, group_rows), group_rows), :] = dot(
            onehot[pl.ds(pl.multiple_of(b * group_rows, group_rows), group_rows), :].astype(BF16), own_lanes
        )

    loads[2].wait()
    loads[3].wait()

    def dequantize(k):
        cols = pl.ds(pl.multiple_of(k * LANES, LANES), LANES)
        scale = scales[:, cols].astype(F32)
        for j in range(groups):
            weight[j * LANES : (j + 1) * LANES, cols] = (
                codes[j * LANES : (j + 1) * LANES, cols].astype(F32) * scale[j : j + 1, :]
            ).astype(BF16)

    each(0, chunks // 2, dequantize)

    def wait_block(i):
        @pl.when(plane_from(i) // HALF == c)
        def _():
            block_copy(i).wait_recv()

    each(1, HOMES, wait_block)

    far = (6, -6, 3, -3)

    def far_copy(n):
        return rcopy(
            tiles.at[c, z], tiles.at[c, z], zg1_s.at[n], zg1_r.at[n], (g, layer(far[n]) * 2 + c)
        )

    near = [(src, step) for src in (0, -6, 6, -3, 3) for step in (1, -1)]

    def near_copy(n):
        src, step = near[n]
        s = layer(src)
        return rcopy(tiles.at[c, s], tiles.at[c, s], zg2_s.at[n], zg2_r.at[n], (g, layer(step) * 2 + c))

    quarter = HALF // 2

    def last_copy(n):
        src, step = ((-6, 2), (6, -2))[n]
        s = layer(src)
        some = tiles.at[c, s, pl.ds(n * quarter, quarter)]
        return rcopy(some, some, zg3_s.at[n], zg3_r.at[n], (g, layer(step) * 2 + c))

    begun = [0] + [-d for d in far] + [src - step for src, step in near] + [8]

    def pass_copy(n):
        some = tiles.at[c, layer(begun[n])]
        return rcopy(some, some, pas_s.at[n], pas_r.at[n], sib)

    for n in range(4):
        far_copy(n).start()
    for n in range(2):
        near_copy(n).start()
    pass_copy(0).start()

    each(chunks // 2, chunks, dequantize)
    each(0, HOMES, own_mask)

    each(1, LAYERS, lambda i: slice_copy(i).wait_recv())
    shuffle[...] = feats[...].astype(F32).reshape(LAYERS * 16, LANES)
    for j in range(lane_width // LANES):
        low_lhs[:, j * LANES : (j + 1) * LANES] = shuffle[
            pl.ds(c * (lane_width // LANES) + j, group_rows, stride=8), :
        ].astype(BF16)

    each(1, HOMES, lambda i: down_copy(i).wait_recv())
    chosen = select[...] * lax.dot_general(
        low_lhs[...],
        got_down[...].reshape(HOMES * rank, lane_width),
        (((1,), (1,)), ((), ())),
        preferred_element_type=F32,
    )
    reduced = chosen[:, :LANES]
    for b in range(1, HOMES * rank // LANES):
        reduced += chosen[:, b * LANES : (b + 1) * LANES]
    reduced += pltpu.roll(reduced, rank, 1)
    low = jnp.where(iota((LAYERS, LANES), 1) < rank, reduced[:LAYERS], reduced[LAYERS:])
    low_sum[...] = low
    low_send[...] = low.astype(BF16)

    def low_copy(i):
        return rcopy(low_send, low_got.at[z], low_s.at[i], low_r.at[i], (g, layer(i) * 2 + c))

    in_order(along, lambda i: low_copy(i).start())

    for n in range(4):
        far_copy(n).wait_recv()
        near_copy(2 + 2 * n).start()
        near_copy(3 + 2 * n).start()
        if n < 2:
            last_copy(n).start()
        pass_copy(1 + n).start()

    low_got[z] = jnp.zeros((LAYERS, LANES), BF16)
    each(1, LAYERS, lambda i: low_copy(i).wait_recv())
    acc = low_sum[...]
    for b in range(LAYERS):
        acc += low_got[b].astype(F32)
    low_sum[...] = acc
    swap_low = rcopy(low_sum, low_sib, sib_s.at[1], sib_r.at[1], sib)
    swap_low.start()
    swap_low.wait_recv()
    red_send[...] = (low_sum[...] + low_sib[...]).astype(BF16)

    def red_copy(i):
        return rcopy(red_send, red.at[g], red_s.at[i], red_r.at[i], (plane(i), t))

    in_order(across, lambda i: red_copy(i).start())
    red[g] = red_send[...]

    for n in range(len(near)):
        near_copy(n).wait_recv()
        pass_copy(5 + n).start()
    last_copy(0).wait_recv()
    last_copy(1).wait_recv()
    pass_copy(15).start()

    for n in range(LAYERS):
        pass_copy(n).wait_recv()

    def arrange(b):
        shuffle[...] = tiles[b // HALF, :, b % HALF].astype(F32).reshape(LAYERS * 16, LANES)
        here = pl.ds(pl.multiple_of(place(b) * group_rows, group_rows), group_rows)
        for j in range(groups):
            lhs[here, j * LANES : (j + 1) * LANES] = shuffle[pl.ds(j, group_rows, stride=8), :].astype(BF16)

    each(0, HOMES, arrange)

    def base(k, width):
        block = dot(lhs[...], weight[:, pl.ds(pl.multiple_of(k * LANES, LANES), width)])
        for i in range(width // LANES):
            total[k + i] = block[:, i * LANES : (i + 1) * LANES]

    each(0, chunks // 2, lambda n: base(2 * n, 2 * LANES))
    if chunks % 2:
        base(chunks - 1, LANES)

    each(1, HOMES, lambda i: red_copy(i).wait_recv())
    spread_from = iota((LANES, 2 * per_home * rank), 0)
    spread_to = iota((LANES, 2 * per_home * rank), 1)
    copies = ones_where(
        spread_from == spread_to % rank + (spread_to // (per_home * rank)) * rank
    )
    wide = per_home * rank
    expand[...] = dot(red[...].reshape(HOMES * LAYERS, LANES), copies)
    for b in range(HOMES):
        here = pl.multiple_of(place(b) * group_rows, group_rows)
        lines = expand[b * LAYERS : (b + 1) * LAYERS, :]
        top = pl.ds(here, LAYERS)
        bottom = pl.ds(pl.multiple_of(here + LAYERS, LAYERS), LAYERS)
        spread[top, :] = (lines[:, :wide] * mask[top, :]).astype(BF16)
        spread[bottom, :] = (lines[:, wide:] * mask[bottom, :]).astype(BF16)

    loads[4].wait()
    first_at = jnp.where(c == 0, x, y)
    second_at = jnp.where(c == 0, y, x)
    four = SIDE * group_rows

    def along_first(d):
        to = lax.rem(first_at + d, SIDE)
        return to, (jnp.where(c == 0, to * SIDE + y, x * SIDE + to), t)

    def along_second(d):
        to = lax.rem(second_at + d, SIDE)
        return to, (jnp.where(c == 0, x * SIDE + to, to * SIDE + y), t)

    def part_copy(k, d):
        to, dev = along_first(d)
        src = part.at[k, pl.ds(pl.multiple_of(to * four, four), four)]
        return rcopy(src, got_part.at[k, d - 1], rs1_s.at[k, d - 1], rs1_r.at[k, d - 1], dev)

    def half_copy(k, d):
        to, dev = along_second(d)
        src = half_sum.at[k, pl.ds(pl.multiple_of(to * group_rows, group_rows), group_rows)]
        return rcopy(src, got_half.at[k, d - 1], rs2_s.at[k, d - 1], rs2_r.at[k, d - 1], dev)

    def send_part(k, width):
        block = dot(spread[...], up[:, pl.ds(pl.multiple_of(k * LANES, LANES), width)])
        for i in range(width // LANES):
            part[k + i] = (total[k + i] + adapter_scale * block[:, i * LANES : (i + 1) * LANES]).astype(BF16)
            for d in range(1, SIDE):
                part_copy(k + i, d).start()

    def send_half(k):
        own = part[k, pl.ds(pl.multiple_of(first_at * four, four), four), :].astype(F32)
        for d in range(1, SIDE):
            part_copy(k, d).wait_recv()
            own += got_part[k, d - 1].astype(F32)
        half_sum[k] = own.astype(BF16)
        for d in range(1, SIDE):
            half_copy(k, d).start()

    lead = 4

    def both(n):
        send_part(2 * n + lead, 2 * LANES)
        send_half(2 * n)
        send_half(2 * n + 1)

    each(0, lead // 2, lambda n: send_part(2 * n, 2 * LANES))
    each(0, (chunks - lead) // 2, both)
    if chunks % 2:
        send_part(chunks - 1, LANES)
    each((chunks - lead) // 2 * 2, chunks, send_half)

    loads[7].wait()
    live = iota((group_rows, LANES), 0) < live_ref[g]

    def finish(k):
        own = half_sum[k, pl.ds(pl.multiple_of(second_at * group_rows, group_rows), group_rows), :].astype(F32)
        for d in range(1, SIDE):
            half_copy(k, d).wait_recv()
            own += got_half[k, d - 1].astype(F32)
        out_ref[:, pl.ds(pl.multiple_of(k * LANES, LANES), LANES)] = jnp.where(live, own, 0.0).astype(BF16)

    each(0, chunks, finish)

    swap.wait_send()
    swap_low.wait_send()

    @pl.when(carrier)
    def _():
        each(1, HOMES, lambda i: block_copy(i).wait_send())

    def sent(i):
        slice_copy(i).wait_send()
        down_copy(i).wait_send()
        low_copy(i).wait_send()
        red_copy(i).wait_send()

    each(1, HOMES, sent)
    for n in range(4):
        far_copy(n).wait_send()
    for n in range(len(near)):
        near_copy(n).wait_send()
    last_copy(0).wait_send()
    last_copy(1).wait_send()
    for n in range(LAYERS):
        pass_copy(n).wait_send()

    def sent_parts(k):
        for d in range(1, SIDE):
            part_copy(k, d).wait_send()
            half_copy(k, d).wait_send()

    each(0, chunks, sent_parts)


def body(tokens, weight_codes, weight_scales, adapter_down, adapter_up, row_adapter, adapter_slot, live_rows):
    width = tokens.shape[1]
    depth, columns = weight_codes.shape
    down = jnp.swapaxes(adapter_down, 1, 2)
    per_home, rank, lane_width = down.shape
    all_rows = row_adapter.shape[0]
    group_rows = all_rows // HOMES
    chunks = columns // LANES
    wide = per_home * rank
    up = adapter_up.reshape(wide, columns)
    rows = row_adapter.reshape(all_rows // LANES, LANES)
    vmem, dma = pltpu.VMEM, pltpu.SemaphoreType.DMA
    scratch = [
        vmem(rows.shape, jnp.int32),
        pltpu.SMEM(adapter_slot.shape, jnp.int32),
        pltpu.SMEM(live_rows.shape, jnp.int32),
        vmem((1, width), BF16),
        vmem((depth, columns), BF16),
        vmem(weight_scales.shape, BF16),
        vmem(down.shape, BF16),
        vmem((wide, columns), BF16),
        vmem((width // LANES, LANES), BF16),
        vmem((width // LANES, LANES), BF16),
        vmem((HOMES, 16, LANES), BF16),
        vmem((2, LAYERS, HALF, 16, LANES), BF16),
        vmem((LAYERS, 16, LANES), BF16),
        vmem((all_rows, HOMES * per_home), F32),
        vmem((HOMES, per_home * lane_width), F32),
        vmem((HOMES, rank, lane_width), BF16),
        vmem((HOMES, rank, lane_width), BF16),
        vmem((depth, columns), BF16),
        vmem((LAYERS * 16, LANES), F32),
        vmem((all_rows, depth), BF16),
        vmem((group_rows, lane_width), BF16),
        vmem((group_rows, HOMES * rank), F32),
        vmem((LAYERS, LANES), BF16),
        vmem((LAYERS, LAYERS, LANES), BF16),
        vmem((LAYERS, LANES), F32),
        vmem((LAYERS, LANES), F32),
        vmem((LAYERS, LANES), BF16),
        vmem((HOMES, LAYERS, LANES), BF16),
        vmem((HOMES * LAYERS, 2 * wide), F32),
        vmem((all_rows, wide), BF16),
        vmem((all_rows, wide), F32),
        vmem((chunks, all_rows, LANES), F32),
        vmem((chunks, all_rows, LANES), BF16),
        vmem((chunks, SIDE - 1, SIDE * group_rows, LANES), BF16),
        vmem((chunks, SIDE * group_rows, LANES), BF16),
        vmem((chunks, SIDE - 1, group_rows, LANES), BF16),
        dma((8,)),
        dma((3,)),
        dma((3,)),
    ]
    for count in (HOMES, LAYERS, HOMES, 4, 10, 2, LAYERS, LAYERS, HOMES):
        scratch += [dma((count,)), dma((count,))]
    scratch += [dma((chunks, SIDE - 1))] * 4
    return pl.pallas_call(
        kernel,
        out_shape=jax.ShapeDtypeStruct((group_rows, columns), BF16),
        in_specs=[pl.BlockSpec(memory_space=pltpu.HBM)] * 8,
        out_specs=pl.BlockSpec(memory_space=pltpu.VMEM),
        scratch_shapes=scratch,
        compiler_params=pltpu.CompilerParams(
            collective_id=0, has_side_effects=True, vmem_limit_bytes=60 * 1024 * 1024
        ),
    )(tokens, weight_codes, weight_scales, down, up, rows, adapter_slot, live_rows)


def solution(mesh):
    in_specs = (
        P(("req", "tp"), None),
        P("req", "tp"),
        P("req", "tp"),
        P("req", "tp", None),
        P("req", None, "tp"),
        P(),
        P(),
        P(),
    )
    return jax.shard_map(body, mesh=mesh, in_specs=in_specs, out_specs=P("req", "tp"), check_vma=False)
```

```python
import functools

import jax
import jax.numpy as jnp
from jax import lax
from jax.experimental import pallas as pl
from jax.experimental.pallas import tpu as pltpu
from jax.sharding import PartitionSpec as P

MESH = pl.DeviceIdType.MESH
F32 = jnp.float32
BF16 = jnp.bfloat16
LANES = 128
SIDE = 4
HOMES = SIDE * SIDE
LAYERS = 16
HALF = HOMES // 2
adapter_scale = 2.0


def iota(shape, axis):
    return lax.broadcasted_iota(jnp.int32, shape, axis)


def ones_where(mask, dtype=BF16):
    return jnp.where(mask, 1.0, 0.0).astype(dtype)


def dot(a, b):
    return jnp.dot(a, b, preferred_element_type=F32)


def kernel(
    tok_hbm,
    codes_hbm,
    scales_hbm,
    down_hbm,
    up_hbm,
    row_hbm,
    slot_hbm,
    live_hbm,
    out_ref,
    row_ref,
    slot_ref,
    live_ref,
    tok,
    codes,
    scales,
    down,
    up,
    mine,
    other,
    pairs,
    tiles,
    feats,
    onehot,
    wanted,
    send_down,
    got_down,
    weight,
    shuffle,
    lhs,
    low_lhs,
    select,
    low_send,
    low_got,
    low_sum,
    low_sib,
    red_send,
    red,
    expand,
    spread,
    mask,
    total,
    part,
    got_part,
    half_sum,
    got_half,
    load_sem,
    sib_s,
    sib_r,
    blk_s,
    blk_r,
    slc_s,
    slc_r,
    dwn_s,
    dwn_r,
    zg1_s,
    zg1_r,
    zg2_s,
    zg2_r,
    zg3_s,
    zg3_r,
    pas_s,
    pas_r,
    low_s,
    low_r,
    red_s,
    red_r,
    rs1_s,
    rs1_r,
    rs2_s,
    rs2_r,
):
    g = lax.axis_index("req")
    t = lax.axis_index("tp")
    x, y = g // SIDE, g % SIDE
    z, c = t // 2, t % 2
    sib = (g, z * 2 + 1 - c)
    depth, columns = weight.shape
    chunks = columns // LANES
    groups = depth // LANES
    per_home, rank, lane_width = down.shape
    adapters = HOMES * per_home
    group_rows = 2 * LAYERS

    def plane(i):
        return lax.rem(x + i // SIDE, SIDE) * SIDE + lax.rem(y + i % SIDE, SIDE)

    def plane_from(i):
        return lax.rem(x + SIDE - i // SIDE, SIDE) * SIDE + lax.rem(y + SIDE - i % SIDE, SIDE)

    def layer(i):
        return lax.rem(z + i + LAYERS, LAYERS)

    def rcopy(src, dst, ss, rs, dev):
        return pltpu.make_async_remote_copy(
            src_ref=src, dst_ref=dst, send_sem=ss, recv_sem=rs, device_id=dev, device_id_type=MESH
        )

    early = 4
    across = (10, 9, 11, 6, 14, 5, 7, 13, 15, 8, 2, 1, 3, 4, 12)
    along = (8, 7, 9, 6, 10, 5, 11, 4, 12, 3, 13, 2, 14, 1, 15)

    def in_order(order, fn):
        for i in order:
            fn(i)

    def arrived(ref, sem):
        rcopy(ref, ref, sem, sem, sib).wait_recv()

    def left(ref, sem):
        rcopy(ref, ref, sem, sem, sib).wait_send()

    def each(lo, hi, fn):
        def step(i, carry):
            fn(i)
            return carry

        lax.fori_loop(lo, hi, step, 0)

    barrier = pltpu.get_barrier_semaphore()

    def greet(i):
        pl.semaphore_signal(barrier, inc=1, device_id=(plane(i), t), device_id_type=MESH)
        pl.semaphore_signal(barrier, inc=1, device_id=(g, layer(i) * 2 + c), device_id_type=MESH)

    pl.semaphore_signal(barrier, inc=1, device_id=sib, device_id_type=MESH)
    each(1, HOMES, greet)

    loads = [
        pltpu.make_async_copy(src, dst, load_sem.at[i])
        for i, (src, dst) in enumerate(
            [
                (tok_hbm, tok),
                (down_hbm, down),
                (codes_hbm, codes),
                (scales_hbm, scales),
                (up_hbm, up),
                (row_hbm, row_ref),
                (slot_hbm, slot_ref),
                (live_hbm, live_ref),
            ]
        )
    ]
    for i in (5, 6, 1, 0):
        loads[i].start()

    loads[0].wait()
    row = tok[...].astype(F32)
    for b in range(mine.shape[0] // 16):
        mine[b * 16 : (b + 1) * 16, :] = jnp.concatenate(
            [row[:, (b * 16 + i) * LANES : (b * 16 + i + 1) * LANES] for i in range(16)], axis=0
        ).astype(BF16)

    loads[5].wait()
    loads[6].wait()
    rows = row_ref[...]
    slots = jnp.zeros_like(rows)
    for a in range(adapters):
        slots = jnp.where(rows == a, slot_ref[a], slots)
    eye = ones_where(iota((adapters, adapters), 0) == iota((adapters, adapters), 1))
    for b in range(rows.shape[0]):
        hit = ones_where(slots[b : b + 1, :] == iota((adapters, LANES), 0))
        onehot[b * LANES : (b + 1) * LANES, :] = lax.dot_general(
            hit, eye, (((0,), (0,)), ((), ())), preferred_element_type=F32
        )
    all_rows = onehot.shape[0]
    in_group = ones_where(iota((HOMES, all_rows), 1) // group_rows == iota((HOMES, all_rows), 0))
    named = dot(in_group, onehot[...].astype(BF16))
    pick = ones_where(
        iota((adapters, per_home * lane_width), 0)
        == g * per_home + iota((adapters, per_home * lane_width), 1) // lane_width
    )
    wanted[...] = jnp.where(dot(named.astype(BF16), pick) > 0, 1.0, 0.0)

    loads[1].wait()

    def choose(b):
        line = wanted[pl.ds(b, 1), :]
        weights = [
            jnp.broadcast_to(line[:, a * lane_width : (a + 1) * lane_width], (16, lane_width)).astype(BF16)
            for a in range(per_home)
        ]
        for i in range(rank // 16):
            lines = slice(i * 16, (i + 1) * 16)
            block = down[0, lines, :] * weights[0]
            for a in range(1, per_home):
                block += down[a, lines, :] * weights[a]
            send_down[b, lines, :] = block

    each(0, HOMES, choose)
    for i in (2, 3, 4, 7):
        loads[i].start()

    pl.semaphore_wait(barrier, 2 * (HOMES - 1) + 1)

    def down_copy(i):
        b = plane(i)
        return rcopy(send_down.at[b], got_down.at[g], dwn_s.at[0], dwn_r.at[0], (b, t))

    swap = rcopy(mine, other, sib_s.at[0], sib_r.at[0], sib)
    swap.start()
    in_order(across[:early], lambda i: down_copy(i).start())
    swap.wait_recv()
    for b in range(HOMES // 2):
        own = mine[b * 16 : (b + 1) * 16, :].astype(F32)
        theirs = other[b * 16 : (b + 1) * 16, :].astype(F32)
        first = jnp.where(c == 0, own, theirs)
        second = jnp.where(c == 0, theirs, own)
        pairs[2 * b] = jnp.concatenate([first[:8], second[:8]], axis=0).astype(BF16)
        pairs[2 * b + 1] = jnp.concatenate([first[8:], second[8:]], axis=0).astype(BF16)

    carrier = g // HALF == c

    def block_copy(i):
        b = plane(i)
        return rcopy(pairs.at[b], tiles.at[c, z, g % HALF], blk_s.at[0], blk_r.at[0], (b, t))

    def slice_copy(i):
        d = layer(i)
        return rcopy(pairs.at[d], feats.at[z], slc_s.at[0], slc_r.at[0], (g, d * 2 + c))

    @pl.when(carrier)
    def _():
        in_order(across, lambda i: block_copy(i).start())
        tiles[c, z, g % HALF] = pairs[g]

    in_order(along, lambda i: slice_copy(i).start())
    feats[z] = pairs[z]
    in_order(across[early:], lambda i: down_copy(i).start())
    got_down[g] = send_down[g]

    by_home = ones_where(iota((adapters, HOMES * rank), 0) // per_home == iota((adapters, HOMES * rank), 1) // rank)
    select[...] = dot(onehot[pl.ds(pl.multiple_of(g * group_rows, group_rows), group_rows), :].astype(BF16), by_home)

    def place(b):
        return jnp.where(c == 0, b, (b % SIDE) * SIDE + b // SIDE)

    own_lanes = ones_where(
        iota((adapters, per_home * rank), 0) == g * per_home + iota((adapters, per_home * rank), 1) // rank
    )

    def own_mask(b):
        mask[pl.ds(pl.multiple_of(place(b) * group_rows, group_rows), group_rows), :] = dot(
            onehot[pl.ds(pl.multiple_of(b * group_rows, group_rows), group_rows), :].astype(BF16), own_lanes
        )

    loads[2].wait()
    loads[3].wait()

    def dequantize(k):
        cols = pl.ds(pl.multiple_of(k * LANES, LANES), LANES)
        scale = scales[:, cols].astype(F32)
        for j in range(groups):
            weight[j * LANES : (j + 1) * LANES, cols] = (
                codes[j * LANES : (j + 1) * LANES, cols].astype(F32) * scale[j : j + 1, :]
            ).astype(BF16)

    each(0, chunks // 2, dequantize)

    @pl.when(carrier)
    def _():
        arrived(tiles.at[c, z, pl.ds(0, HALF - 1)], blk_r.at[0])

    @pl.when(jnp.logical_not(carrier))
    def _():
        arrived(tiles.at[c, z], blk_r.at[0])


    far = (6, -6, 3, -3)

    def far_copy(n):
        return rcopy(
            tiles.at[c, z], tiles.at[c, z], zg1_s.at[0], zg1_r.at[n], (g, layer(far[n]) * 2 + c)
        )

    near = [(src, step) for src in (0, -6, 6, -3, 3) for step in (1, -1)]

    def near_copy(n):
        src, step = near[n]
        s = layer(src)
        return rcopy(tiles.at[c, s], tiles.at[c, s], zg2_s.at[0], zg2_r.at[n // 2], (g, layer(step) * 2 + c))

    quarter = HALF // 2

    def last_copy(n):
        src, step = ((-6, 2), (6, -2))[n]
        s = layer(src)
        some = tiles.at[c, s, pl.ds(n * quarter, quarter)]
        return rcopy(some, some, zg3_s.at[0], zg3_r.at[0], (g, layer(step) * 2 + c))

    begun = [0] + [-d for d in far] + [src - step for src, step in near] + [8]

    def pass_copy(n):
        some = tiles.at[c, layer(begun[n])]
        return rcopy(some, some, pas_s.at[0], pas_r.at[0], sib)

    for n in range(4):
        far_copy(n).start()
    for n in range(2):
        near_copy(n).start()
    pass_copy(0).start()

    each(chunks // 2, chunks, dequantize)
    each(0, HOMES, own_mask)

    arrived(feats.at[pl.ds(0, LAYERS - 1)], slc_r.at[0])
    shuffle[...] = feats[...].astype(F32).reshape(LAYERS * 16, LANES)
    for j in range(lane_width // LANES):
        low_lhs[:, j * LANES : (j + 1) * LANES] = shuffle[
            pl.ds(c * (lane_width // LANES) + j, group_rows, stride=8), :
        ].astype(BF16)

    arrived(got_down.at[pl.ds(0, HOMES - 1)], dwn_r.at[0])
    chosen = select[...] * lax.dot_general(
        low_lhs[...],
        got_down[...].reshape(HOMES * rank, lane_width),
        (((1,), (1,)), ((), ())),
        preferred_element_type=F32,
    )
    reduced = chosen[:, :LANES]
    for b in range(1, HOMES * rank // LANES):
        reduced += chosen[:, b * LANES : (b + 1) * LANES]
    reduced += pltpu.roll(reduced, rank, 1)
    low = jnp.where(iota((LAYERS, LANES), 1) < rank, reduced[:LAYERS], reduced[LAYERS:])
    low_sum[...] = low
    low_send[...] = low.astype(BF16)

    def low_copy(i):
        return rcopy(low_send, low_got.at[z], low_s.at[0], low_r.at[0], (g, layer(i) * 2 + c))

    in_order(along, lambda i: low_copy(i).start())

    for n in range(4):
        far_copy(n).wait_recv()
        near_copy(2 + 2 * n).start()
        near_copy(3 + 2 * n).start()
        if n < 2:
            last_copy(n).start()
        pass_copy(1 + n).start()

    low_got[z] = jnp.zeros((LAYERS, LANES), BF16)
    arrived(low_got.at[pl.ds(0, LAYERS - 1)], low_r.at[0])
    acc = low_sum[...]
    for b in range(LAYERS):
        acc += low_got[b].astype(F32)
    low_sum[...] = acc
    swap_low = rcopy(low_sum, low_sib, sib_s.at[1], sib_r.at[1], sib)
    swap_low.start()
    swap_low.wait_recv()
    red_send[...] = (low_sum[...] + low_sib[...]).astype(BF16)

    def red_copy(i):
        return rcopy(red_send, red.at[g], red_s.at[0], red_r.at[0], (plane(i), t))

    in_order(across, lambda i: red_copy(i).start())
    red[g] = red_send[...]

    for n in range(0, len(near), 2):
        arrived(tiles.at[c, pl.ds(0, 2)], zg2_r.at[n // 2])
        pass_copy(5 + n).start()
        pass_copy(6 + n).start()
    arrived(tiles.at[c, 0], zg3_r.at[0])
    pass_copy(15).start()
    arrived(tiles.at[1 - c], pas_r.at[0])

    def arrange(b):
        shuffle[...] = tiles[b // HALF, :, b % HALF].astype(F32).reshape(LAYERS * 16, LANES)
        here = pl.ds(pl.multiple_of(place(b) * group_rows, group_rows), group_rows)
        for j in range(groups):
            lhs[here, j * LANES : (j + 1) * LANES] = shuffle[pl.ds(j, group_rows, stride=8), :].astype(BF16)

    each(0, HOMES, arrange)

    pair = 2 * LANES
    spans = [(k, min(pair, columns - k * LANES)) for k in range(0, chunks, 2)]

    def base(j, k, width):
        total[j, :, :width] = dot(lhs[...], weight[:, k * LANES : k * LANES + width])

    for j, (k, width) in enumerate(spans):
        base(j, k, width)

    arrived(red.at[pl.ds(0, HOMES - 1)], red_r.at[0])
    spread_from = iota((LANES, 2 * per_home * rank), 0)
    spread_to = iota((LANES, 2 * per_home * rank), 1)
    copies = ones_where(
        spread_from == spread_to % rank + (spread_to // (per_home * rank)) * rank
    )
    wide = per_home * rank
    expand[...] = dot(red[...].reshape(HOMES * LAYERS, LANES), copies)
    for b in range(HOMES):
        here = pl.multiple_of(place(b) * group_rows, group_rows)
        lines = expand[b * LAYERS : (b + 1) * LAYERS, :]
        top = pl.ds(here, LAYERS)
        bottom = pl.ds(pl.multiple_of(here + LAYERS, LAYERS), LAYERS)
        spread[top, :] = (lines[:, :wide] * mask[top, :]).astype(BF16)
        spread[bottom, :] = (lines[:, wide:] * mask[bottom, :]).astype(BF16)

    loads[4].wait()
    first_at = jnp.where(c == 0, x, y)
    second_at = jnp.where(c == 0, y, x)
    four = SIDE * group_rows

    def along_first(d):
        to = lax.rem(first_at + d, SIDE)
        return to, (jnp.where(c == 0, to * SIDE + y, x * SIDE + to), t)

    def along_second(d):
        to = lax.rem(second_at + d, SIDE)
        return to, (jnp.where(c == 0, x * SIDE + to, to * SIDE + y), t)

    def part_copy(j, d):
        to, dev = along_first(d)
        lanes = pl.ds(0, spans[j][1])
        src = part.at[j, pl.ds(pl.multiple_of(to * four, four), four), lanes]
        return rcopy(src, got_part.at[j, d - 1, :, lanes], rs1_s.at[0], rs1_r.at[j], dev)

    def half_copy(j, d):
        to, dev = along_second(d)
        lanes = pl.ds(0, spans[j][1])
        src = half_sum.at[j, pl.ds(pl.multiple_of(to * group_rows, group_rows), group_rows), lanes]
        return rcopy(src, got_half.at[j, d - 1, :, lanes], rs2_s.at[0], rs2_r.at[j], dev)

    def send_part(j):
        k, width = spans[j]
        block = adapter_scale * dot(spread[...], up[:, k * LANES : k * LANES + width])
        part[j, :, :width] = (total[j, :, :width] + block).astype(BF16)
        for d in range(1, SIDE):
            part_copy(j, d).start()

    def send_half(j):
        k, width = spans[j]
        arrived(got_part.at[j, :, :, pl.ds(0, width)], rs1_r.at[j])
        own = part[j, pl.ds(pl.multiple_of(first_at * four, four), four), :width].astype(F32)
        for d in range(1, SIDE):
            own += got_part[j, d - 1, :, :width].astype(F32)
        half_sum[j, :, :width] = own.astype(BF16)
        for d in range(1, SIDE):
            half_copy(j, d).start()

    lead = 2
    for j in range(len(spans) + lead):
        if j < len(spans):
            send_part(j)
        if j >= lead:
            send_half(j - lead)

    loads[7].wait()
    live = iota((group_rows, pair), 0) < live_ref[g]

    for j, (k, width) in enumerate(spans):
        arrived(got_half.at[j, :, :, pl.ds(0, width)], rs2_r.at[j])
        own = half_sum[j, pl.ds(pl.multiple_of(second_at * group_rows, group_rows), group_rows), :width].astype(F32)
        for d in range(1, SIDE):
            own += got_half[j, d - 1, :, :width].astype(F32)
        out_ref[:, k * LANES : k * LANES + width] = jnp.where(live[:, :width], own, 0.0).astype(BF16)

    swap.wait_send()
    swap_low.wait_send()

    @pl.when(carrier)
    def _():
        left(feats.at[pl.ds(0, HOMES - 1)], blk_s.at[0])

    left(feats.at[pl.ds(0, LAYERS - 1)], slc_s.at[0])
    left(got_down.at[pl.ds(0, HOMES - 1)], dwn_s.at[0])
    left(low_got.at[pl.ds(0, LAYERS - 1)], low_s.at[0])
    left(red.at[pl.ds(0, HOMES - 1)], red_s.at[0])
    left(tiles.at[c, pl.ds(0, len(far))], zg1_s.at[0])
    left(tiles.at[c, pl.ds(0, len(near))], zg2_s.at[0])
    left(tiles.at[c, 0], zg3_s.at[0])
    left(tiles.at[c], pas_s.at[0])
    for j, (k, width) in enumerate(spans):
        left(got_part.at[j, :, :, pl.ds(0, width)], rs1_s.at[0])
        left(got_half.at[j, :, :, pl.ds(0, width)], rs2_s.at[0])


def body(tokens, weight_codes, weight_scales, adapter_down, adapter_up, row_adapter, adapter_slot, live_rows):
    width = tokens.shape[1]
    depth, columns = weight_codes.shape
    down = jnp.swapaxes(adapter_down, 1, 2)
    per_home, rank, lane_width = down.shape
    all_rows = row_adapter.shape[0]
    group_rows = all_rows // HOMES
    chunks = columns // LANES
    wide = per_home * rank
    pairs = (chunks + 1) // 2
    up = adapter_up.reshape(wide, columns)
    rows = row_adapter.reshape(all_rows // LANES, LANES)
    vmem, dma = pltpu.VMEM, pltpu.SemaphoreType.DMA
    scratch = [
        vmem(rows.shape, jnp.int32),
        pltpu.SMEM(adapter_slot.shape, jnp.int32),
        pltpu.SMEM(live_rows.shape, jnp.int32),
        vmem((1, width), BF16),
        vmem((depth, columns), BF16),
        vmem(weight_scales.shape, BF16),
        vmem(down.shape, BF16),
        vmem((wide, columns), BF16),
        vmem((width // LANES, LANES), BF16),
        vmem((width // LANES, LANES), BF16),
        vmem((HOMES, 16, LANES), BF16),
        vmem((2, LAYERS, HALF, 16, LANES), BF16),
        vmem((LAYERS, 16, LANES), BF16),
        vmem((all_rows, HOMES * per_home), F32),
        vmem((HOMES, per_home * lane_width), F32),
        vmem((HOMES, rank, lane_width), BF16),
        vmem((HOMES, rank, lane_width), BF16),
        vmem((depth, columns), BF16),
        vmem((LAYERS * 16, LANES), F32),
        vmem((all_rows, depth), BF16),
        vmem((group_rows, lane_width), BF16),
        vmem((group_rows, HOMES * rank), F32),
        vmem((LAYERS, LANES), BF16),
        vmem((LAYERS, LAYERS, LANES), BF16),
        vmem((LAYERS, LANES), F32),
        vmem((LAYERS, LANES), F32),
        vmem((LAYERS, LANES), BF16),
        vmem((HOMES, LAYERS, LANES), BF16),
        vmem((HOMES * LAYERS, 2 * wide), F32),
        vmem((all_rows, wide), BF16),
        vmem((all_rows, wide), F32),
        vmem((pairs, all_rows, 2 * LANES), F32),
        vmem((pairs, all_rows, 2 * LANES), BF16),
        vmem((pairs, SIDE - 1, SIDE * group_rows, 2 * LANES), BF16),
        vmem((pairs, SIDE * group_rows, 2 * LANES), BF16),
        vmem((pairs, SIDE - 1, group_rows, 2 * LANES), BF16),
        dma((8,)),
        dma((2,)),
        dma((2,)),
    ]
    for count in (1, 1, 1, 4, 5, 1, 1, 1, 1, pairs, pairs):
        scratch += [dma((1,)), dma((count,))]
    return pl.pallas_call(
        kernel,
        out_shape=jax.ShapeDtypeStruct((group_rows, columns), BF16),
        in_specs=[pl.BlockSpec(memory_space=pltpu.HBM)] * 8,
        out_specs=pl.BlockSpec(memory_space=pltpu.VMEM),
        scratch_shapes=scratch,
        compiler_params=pltpu.CompilerParams(
            collective_id=0, has_side_effects=True, vmem_limit_bytes=60 * 1024 * 1024
        ),
    )(tokens, weight_codes, weight_scales, down, up, rows, adapter_slot, live_rows)


def solution(mesh):
    in_specs = (
        P(("req", "tp"), None),
        P("req", "tp"),
        P("req", "tp"),
        P("req", "tp", None),
        P("req", None, "tp"),
        P(),
        P(),
        P(),
    )
    return jax.shard_map(body, mesh=mesh, in_specs=in_specs, out_specs=P("req", "tp"), check_vma=False)
```

```python
import functools

import jax
import jax.numpy as jnp
from jax import lax
from jax.experimental import pallas as pl
from jax.experimental.pallas import tpu as pltpu
from jax.sharding import PartitionSpec as P

MESH = pl.DeviceIdType.MESH
F32 = jnp.float32
BF16 = jnp.bfloat16
LANES = 128
SIDE = 4
HOMES = SIDE * SIDE
LAYERS = 16
HALF = HOMES // 2
adapter_scale = 2.0


def iota(shape, axis):
    return lax.broadcasted_iota(jnp.int32, shape, axis)


def ones_where(mask, dtype=BF16):
    return jnp.where(mask, 1.0, 0.0).astype(dtype)


def dot(a, b):
    return jnp.dot(a, b, preferred_element_type=F32)


def kernel(
    tok_hbm,
    codes_hbm,
    scales_hbm,
    down_hbm,
    up_hbm,
    row_hbm,
    slot_hbm,
    live_hbm,
    out_ref,
    row_ref,
    slot_ref,
    live_ref,
    tok,
    codes,
    scales,
    down,
    up,
    mine,
    other,
    pairs,
    tiles,
    feats,
    onehot,
    wanted,
    send_down,
    got_down,
    weight,
    shuffle,
    lhs,
    low_lhs,
    select,
    low_send,
    low_got,
    low_sum,
    low_sib,
    red_send,
    red,
    expand,
    spread,
    mask,
    total,
    part,
    got_part,
    half_sum,
    got_half,
    load_sem,
    sib_s,
    sib_r,
    blk_s,
    blk_r,
    slc_s,
    slc_r,
    dwn_s,
    dwn_r,
    zg1_s,
    zg1_r,
    zg2_s,
    zg2_r,
    zg3_s,
    zg3_r,
    pas_s,
    pas_r,
    low_s,
    low_r,
    red_s,
    red_r,
    rs1_s,
    rs1_r,
    rs2_s,
    rs2_r,
):
    g = lax.axis_index("req")
    t = lax.axis_index("tp")
    x, y = g // SIDE, g % SIDE
    z, c = t // 2, t % 2
    sib = (g, z * 2 + 1 - c)
    depth, columns = weight.shape
    chunks = columns // LANES
    groups = depth // LANES
    per_home, rank, lane_width = down.shape
    adapters = HOMES * per_home
    group_rows = 2 * LAYERS

    def plane(i):
        return lax.rem(x + i // SIDE, SIDE) * SIDE + lax.rem(y + i % SIDE, SIDE)

    def plane_from(i):
        return lax.rem(x + SIDE - i // SIDE, SIDE) * SIDE + lax.rem(y + SIDE - i % SIDE, SIDE)

    def layer(i):
        return lax.rem(z + i + LAYERS, LAYERS)

    def rcopy(src, dst, ss, rs, dev):
        return pltpu.make_async_remote_copy(
            src_ref=src, dst_ref=dst, send_sem=ss, recv_sem=rs, device_id=dev, device_id_type=MESH
        )

    early = 4
    across = (10, 9, 11, 6, 14, 5, 7, 13, 15, 8, 2, 1, 3, 4, 12)
    along = (8, 7, 9, 6, 10, 5, 11, 4, 12, 3, 13, 2, 14, 1, 15)

    def in_order(order, fn):
        for i in order:
            fn(i)

    def arrived(ref, sem):
        rcopy(ref, ref, sem, sem, sib).wait_recv()

    def left(ref, sem):
        rcopy(ref, ref, sem, sem, sib).wait_send()

    def each(lo, hi, fn):
        def step(i, carry):
            fn(i)
            return carry

        lax.fori_loop(lo, hi, step, 0)

    barrier = pltpu.get_barrier_semaphore()

    def greet(i):
        pl.semaphore_signal(barrier, inc=1, device_id=(plane(i), t), device_id_type=MESH)
        pl.semaphore_signal(barrier, inc=1, device_id=(g, layer(i) * 2 + c), device_id_type=MESH)

    pl.semaphore_signal(barrier, inc=1, device_id=sib, device_id_type=MESH)
    each(1, HOMES, greet)

    loads = [
        pltpu.make_async_copy(src, dst, load_sem.at[i])
        for i, (src, dst) in enumerate(
            [
                (tok_hbm, tok),
                (down_hbm, down),
                (codes_hbm, codes),
                (scales_hbm, scales),
                (up_hbm, up),
                (row_hbm, row_ref),
                (slot_hbm, slot_ref),
                (live_hbm, live_ref),
            ]
        )
    ]
    for i in (5, 6, 1, 0):
        loads[i].start()

    loads[0].wait()
    row = tok[...].astype(F32)
    for b in range(mine.shape[0] // 16):
        mine[b * 16 : (b + 1) * 16, :] = jnp.concatenate(
            [row[:, (b * 16 + i) * LANES : (b * 16 + i + 1) * LANES] for i in range(16)], axis=0
        ).astype(BF16)

    loads[5].wait()
    loads[6].wait()
    rows = row_ref[...]
    slots = jnp.zeros_like(rows)
    for a in range(adapters):
        slots = jnp.where(rows == a, slot_ref[a], slots)
    eye = ones_where(iota((adapters, adapters), 0) == iota((adapters, adapters), 1))
    for b in range(rows.shape[0]):
        hit = ones_where(slots[b : b + 1, :] == iota((adapters, LANES), 0))
        onehot[b * LANES : (b + 1) * LANES, :] = lax.dot_general(
            hit, eye, (((0,), (0,)), ((), ())), preferred_element_type=F32
        )
    all_rows = onehot.shape[0]
    in_group = ones_where(iota((HOMES, all_rows), 1) // group_rows == iota((HOMES, all_rows), 0))
    named = dot(in_group, onehot[...].astype(BF16))
    pick = ones_where(
        iota((adapters, per_home * lane_width), 0)
        == g * per_home + iota((adapters, per_home * lane_width), 1) // lane_width
    )
    wanted[...] = jnp.where(dot(named.astype(BF16), pick) > 0, 1.0, 0.0)

    loads[1].wait()

    def choose(b):
        line = wanted[pl.ds(b, 1), :]
        weights = [
            jnp.broadcast_to(line[:, a * lane_width : (a + 1) * lane_width], (16, lane_width)).astype(BF16)
            for a in range(per_home)
        ]
        for i in range(rank // 16):
            lines = slice(i * 16, (i + 1) * 16)
            block = down[0, lines, :] * weights[0]
            for a in range(1, per_home):
                block += down[a, lines, :] * weights[a]
            send_down[b, lines, :] = block

    each(0, HOMES, choose)
    for i in (2, 3, 4, 7):
        loads[i].start()

    pl.semaphore_wait(barrier, 2 * (HOMES - 1) + 1)

    def down_copy(i):
        b = plane(i)
        return rcopy(send_down.at[b], got_down.at[g], dwn_s.at[0], dwn_r.at[0], (b, t))

    swap = rcopy(mine, other, sib_s.at[0], sib_r.at[0], sib)
    swap.start()
    in_order(across[:early], lambda i: down_copy(i).start())
    swap.wait_recv()
    for b in range(HOMES // 2):
        own = mine[b * 16 : (b + 1) * 16, :].astype(F32)
        theirs = other[b * 16 : (b + 1) * 16, :].astype(F32)
        first = jnp.where(c == 0, own, theirs)
        second = jnp.where(c == 0, theirs, own)
        pairs[2 * b] = jnp.concatenate([first[:8], second[:8]], axis=0).astype(BF16)
        pairs[2 * b + 1] = jnp.concatenate([first[8:], second[8:]], axis=0).astype(BF16)

    carrier = g // HALF == c

    def block_copy(i):
        b = plane(i)
        return rcopy(pairs.at[b], tiles.at[c, z, g % HALF], blk_s.at[0], blk_r.at[0], (b, t))

    def slice_copy(i):
        d = layer(i)
        return rcopy(pairs.at[d], feats.at[z], slc_s.at[0], slc_r.at[0], (g, d * 2 + c))

    @pl.when(carrier)
    def _():
        in_order(across, lambda i: block_copy(i).start())
        tiles[c, z, g % HALF] = pairs[g]

    in_order(along, lambda i: slice_copy(i).start())
    feats[z] = pairs[z]
    in_order(across[early:], lambda i: down_copy(i).start())
    got_down[g] = send_down[g]

    by_home = ones_where(iota((adapters, HOMES * rank), 0) // per_home == iota((adapters, HOMES * rank), 1) // rank)
    select[...] = dot(onehot[pl.ds(pl.multiple_of(g * group_rows, group_rows), group_rows), :].astype(BF16), by_home)

    def place(b):
        return jnp.where(c == 0, b, (b % SIDE) * SIDE + b // SIDE)

    own_lanes = ones_where(
        iota((adapters, per_home * rank), 0) == g * per_home + iota((adapters, per_home * rank), 1) // rank
    )

    def own_mask(b):
        mask[pl.ds(pl.multiple_of(place(b) * group_rows, group_rows), group_rows), :] = dot(
            onehot[pl.ds(pl.multiple_of(b * group_rows, group_rows), group_rows), :].astype(BF16), own_lanes
        )

    loads[2].wait()
    loads[3].wait()

    def dequantize(k):
        cols = pl.ds(pl.multiple_of(k * LANES, LANES), LANES)
        scale = scales[:, cols].astype(F32)
        for j in range(groups):
            weight[j * LANES : (j + 1) * LANES, cols] = (
                codes[j * LANES : (j + 1) * LANES, cols].astype(F32) * scale[j : j + 1, :]
            ).astype(BF16)

    each(0, chunks // 2, dequantize)

    @pl.when(carrier)
    def _():
        arrived(tiles.at[c, z, pl.ds(0, HALF - 1)], blk_r.at[0])

    @pl.when(jnp.logical_not(carrier))
    def _():
        arrived(tiles.at[c, z], blk_r.at[0])


    far = (6, -6, 3, -3)

    def far_copy(n):
        return rcopy(
            tiles.at[c, z], tiles.at[c, z], zg1_s.at[0], zg1_r.at[n], (g, layer(far[n]) * 2 + c)
        )

    near = [(src, step) for src in (0, -6, 6, -3, 3) for step in (1, -1)]

    def near_copy(n):
        src, step = near[n]
        s = layer(src)
        return rcopy(tiles.at[c, s], tiles.at[c, s], zg2_s.at[0], zg2_r.at[n // 2], (g, layer(step) * 2 + c))

    quarter = HALF // 2

    def last_copy(n):
        src, step = ((-6, 2), (6, -2))[n]
        s = layer(src)
        some = tiles.at[c, s, pl.ds(n * quarter, quarter)]
        return rcopy(some, some, zg3_s.at[0], zg3_r.at[0], (g, layer(step) * 2 + c))

    begun = [0] + [-d for d in far] + [src - step for src, step in near] + [8]

    def pass_copy(n):
        some = tiles.at[c, layer(begun[n])]
        return rcopy(some, some, pas_s.at[0], pas_r.at[0], sib)

    for n in range(4):
        far_copy(n).start()
    for n in range(2):
        near_copy(n).start()
    pass_copy(0).start()

    each(chunks // 2, chunks, dequantize)
    each(0, HOMES, own_mask)

    arrived(feats.at[pl.ds(0, LAYERS - 1)], slc_r.at[0])
    shuffle[...] = feats[...].astype(F32).reshape(LAYERS * 16, LANES)
    for j in range(lane_width // LANES):
        low_lhs[:, j * LANES : (j + 1) * LANES] = shuffle[
            pl.ds(c * (lane_width // LANES) + j, group_rows, stride=8), :
        ].astype(BF16)

    arrived(got_down.at[pl.ds(0, HOMES - 1)], dwn_r.at[0])
    chosen = select[...] * lax.dot_general(
        low_lhs[...],
        got_down[...].reshape(HOMES * rank, lane_width),
        (((1,), (1,)), ((), ())),
        preferred_element_type=F32,
    )
    reduced = chosen[:, :LANES]
    for b in range(1, HOMES * rank // LANES):
        reduced += chosen[:, b * LANES : (b + 1) * LANES]
    reduced += pltpu.roll(reduced, rank, 1)
    low = jnp.where(iota((LAYERS, LANES), 1) < rank, reduced[:LAYERS], reduced[LAYERS:])
    low_sum[...] = low
    low_send[...] = low.astype(BF16)

    def low_copy(i):
        return rcopy(low_send, low_got.at[z], low_s.at[0], low_r.at[0], (g, layer(i) * 2 + c))

    in_order(along, lambda i: low_copy(i).start())

    for n in range(4):
        far_copy(n).wait_recv()
        near_copy(2 + 2 * n).start()
        near_copy(3 + 2 * n).start()
        if n < 2:
            last_copy(n).start()
        pass_copy(1 + n).start()

    low_got[z] = jnp.zeros((LAYERS, LANES), BF16)
    arrived(low_got.at[pl.ds(0, LAYERS - 1)], low_r.at[0])
    acc = low_sum[...]
    for b in range(LAYERS):
        acc += low_got[b].astype(F32)
    low_sum[...] = acc
    swap_low = rcopy(low_sum, low_sib, sib_s.at[1], sib_r.at[1], sib)
    swap_low.start()
    swap_low.wait_recv()
    red_send[...] = (low_sum[...] + low_sib[...]).astype(BF16)

    def red_copy(i):
        return rcopy(red_send, red.at[g], red_s.at[0], red_r.at[0], (plane(i), t))

    in_order(across, lambda i: red_copy(i).start())
    red[g] = red_send[...]

    for n in range(0, len(near), 2):
        arrived(tiles.at[c, pl.ds(0, 2)], zg2_r.at[n // 2])
        pass_copy(5 + n).start()
        pass_copy(6 + n).start()
    arrived(tiles.at[c, 0], zg3_r.at[0])
    pass_copy(15).start()
    arrived(tiles.at[1 - c], pas_r.at[0])

    def arrange(b):
        shuffle[...] = tiles[b // HALF, :, b % HALF].astype(F32).reshape(LAYERS * 16, LANES)
        here = pl.ds(pl.multiple_of(place(b) * group_rows, group_rows), group_rows)
        for j in range(groups):
            lhs[here, j * LANES : (j + 1) * LANES] = shuffle[pl.ds(j, group_rows, stride=8), :].astype(BF16)

    each(0, HOMES, arrange)

    pair = 2 * LANES
    spans = [(k, min(pair, columns - k * LANES)) for k in range(0, chunks, 2)]

    def base(j, k, width):
        total[j, :, :width] = dot(lhs[...], weight[:, k * LANES : k * LANES + width])

    for j, (k, width) in enumerate(spans):
        base(j, k, width)

    spread_from = iota((LANES, 2 * per_home * rank), 0)
    spread_to = iota((LANES, 2 * per_home * rank), 1)
    copies = ones_where(
        spread_from == spread_to % rank + (spread_to // (per_home * rank)) * rank
    )
    wide = per_home * rank
    arrived(red.at[pl.ds(0, HOMES - 1)], red_r.at[0])
    expand[...] = dot(red[...].reshape(HOMES * LAYERS, LANES), copies)
    for b in range(HOMES):
        here = pl.multiple_of(place(b) * group_rows, group_rows)
        lines = expand[b * LAYERS : (b + 1) * LAYERS, :]
        top = pl.ds(here, LAYERS)
        bottom = pl.ds(pl.multiple_of(here + LAYERS, LAYERS), LAYERS)
        spread[top, :] = (lines[:, :wide] * mask[top, :]).astype(BF16)
        spread[bottom, :] = (lines[:, wide:] * mask[bottom, :]).astype(BF16)

    loads[4].wait()
    first_at = jnp.where(c == 0, x, y)
    second_at = jnp.where(c == 0, y, x)
    four = SIDE * group_rows

    def along_first(d):
        to = lax.rem(first_at + d, SIDE)
        return to, (jnp.where(c == 0, to * SIDE + y, x * SIDE + to), t)

    def along_second(d):
        to = lax.rem(second_at + d, SIDE)
        return to, (jnp.where(c == 0, x * SIDE + to, to * SIDE + y), t)

    def part_copy(j, d):
        to, dev = along_first(d)
        lanes = pl.ds(0, spans[j][1])
        src = part.at[j, pl.ds(pl.multiple_of(to * four, four), four), lanes]
        return rcopy(src, got_part.at[j, d - 1, :, lanes], rs1_s.at[0], rs1_r.at[j], dev)

    def half_copy(j, d):
        to, dev = along_second(d)
        lanes = pl.ds(0, spans[j][1])
        src = half_sum.at[j, pl.ds(pl.multiple_of(to * group_rows, group_rows), group_rows), lanes]
        return rcopy(src, got_half.at[j, d - 1, :, lanes], rs2_s.at[0], rs2_r.at[j], dev)

    def send_part(j):
        k, width = spans[j]
        block = adapter_scale * dot(spread[...], up[:, k * LANES : k * LANES + width])
        part[j, :, :width] = (total[j, :, :width] + block).astype(BF16)
        for d in (2, 1, 3):
            part_copy(j, d).start()

    def send_half(j):
        k, width = spans[j]
        arrived(got_part.at[j, :, :, pl.ds(0, width)], rs1_r.at[j])
        own = part[j, pl.ds(pl.multiple_of(first_at * four, four), four), :width].astype(F32)
        for d in range(1, SIDE):
            own += got_part[j, d - 1, :, :width].astype(F32)
        half_sum[j, :, :width] = own.astype(BF16)
        for d in (2, 1, 3):
            half_copy(j, d).start()

    lead = 3
    for j in range(len(spans) + lead):
        if j < len(spans):
            send_part(j)
        if j >= lead:
            send_half(j - lead)

    loads[7].wait()
    live = iota((group_rows, pair), 0) < live_ref[g]

    for j, (k, width) in enumerate(spans):
        arrived(got_half.at[j, :, :, pl.ds(0, width)], rs2_r.at[j])
        own = half_sum[j, pl.ds(pl.multiple_of(second_at * group_rows, group_rows), group_rows), :width].astype(F32)
        for d in range(1, SIDE):
            own += got_half[j, d - 1, :, :width].astype(F32)
        out_ref[:, k * LANES : k * LANES + width] = jnp.where(live[:, :width], own, 0.0).astype(BF16)

    swap.wait_send()
    swap_low.wait_send()

    @pl.when(carrier)
    def _():
        left(feats.at[pl.ds(0, HOMES - 1)], blk_s.at[0])

    left(feats.at[pl.ds(0, LAYERS - 1)], slc_s.at[0])
    left(got_down.at[pl.ds(0, HOMES - 1)], dwn_s.at[0])
    left(low_got.at[pl.ds(0, LAYERS - 1)], low_s.at[0])
    left(red.at[pl.ds(0, HOMES - 1)], red_s.at[0])
    left(tiles.at[c, pl.ds(0, len(far))], zg1_s.at[0])
    left(tiles.at[c, pl.ds(0, len(near))], zg2_s.at[0])
    left(tiles.at[c, 0], zg3_s.at[0])
    left(tiles.at[c], pas_s.at[0])
    for j, (k, width) in enumerate(spans):
        left(got_part.at[j, :, :, pl.ds(0, width)], rs1_s.at[0])
        left(got_half.at[j, :, :, pl.ds(0, width)], rs2_s.at[0])


def body(tokens, weight_codes, weight_scales, adapter_down, adapter_up, row_adapter, adapter_slot, live_rows):
    width = tokens.shape[1]
    depth, columns = weight_codes.shape
    down = jnp.swapaxes(adapter_down, 1, 2)
    per_home, rank, lane_width = down.shape
    all_rows = row_adapter.shape[0]
    group_rows = all_rows // HOMES
    chunks = columns // LANES
    wide = per_home * rank
    pairs = (chunks + 1) // 2
    up = adapter_up.reshape(wide, columns)
    rows = row_adapter.reshape(all_rows // LANES, LANES)
    vmem, dma = pltpu.VMEM, pltpu.SemaphoreType.DMA
    scratch = [
        vmem(rows.shape, jnp.int32),
        pltpu.SMEM(adapter_slot.shape, jnp.int32),
        pltpu.SMEM(live_rows.shape, jnp.int32),
        vmem((1, width), BF16),
        vmem((depth, columns), BF16),
        vmem(weight_scales.shape, BF16),
        vmem(down.shape, BF16),
        vmem((wide, columns), BF16),
        vmem((width // LANES, LANES), BF16),
        vmem((width // LANES, LANES), BF16),
        vmem((HOMES, 16, LANES), BF16),
        vmem((2, LAYERS, HALF, 16, LANES), BF16),
        vmem((LAYERS, 16, LANES), BF16),
        vmem((all_rows, HOMES * per_home), F32),
        vmem((HOMES, per_home * lane_width), F32),
        vmem((HOMES, rank, lane_width), BF16),
        vmem((HOMES, rank, lane_width), BF16),
        vmem((depth, columns), BF16),
        vmem((LAYERS * 16, LANES), F32),
        vmem((all_rows, depth), BF16),
        vmem((group_rows, lane_width), BF16),
        vmem((group_rows, HOMES * rank), F32),
        vmem((LAYERS, LANES), BF16),
        vmem((LAYERS, LAYERS, LANES), BF16),
        vmem((LAYERS, LANES), F32),
        vmem((LAYERS, LANES), F32),
        vmem((LAYERS, LANES), BF16),
        vmem((HOMES, LAYERS, LANES), BF16),
        vmem((HOMES * LAYERS, 2 * wide), F32),
        vmem((all_rows, wide), BF16),
        vmem((all_rows, wide), F32),
        vmem((pairs, all_rows, 2 * LANES), F32),
        vmem((pairs, all_rows, 2 * LANES), BF16),
        vmem((pairs, SIDE - 1, SIDE * group_rows, 2 * LANES), BF16),
        vmem((pairs, SIDE * group_rows, 2 * LANES), BF16),
        vmem((pairs, SIDE - 1, group_rows, 2 * LANES), BF16),
        dma((8,)),
        dma((2,)),
        dma((2,)),
    ]
    for count in (1, 1, 1, 4, 5, 1, 1, 1, 1, pairs, pairs):
        scratch += [dma((1,)), dma((count,))]
    return pl.pallas_call(
        kernel,
        out_shape=jax.ShapeDtypeStruct((group_rows, columns), BF16),
        in_specs=[pl.BlockSpec(memory_space=pltpu.HBM)] * 8,
        out_specs=pl.BlockSpec(memory_space=pltpu.VMEM),
        scratch_shapes=scratch,
        compiler_params=pltpu.CompilerParams(
            collective_id=0, has_side_effects=True, vmem_limit_bytes=60 * 1024 * 1024
        ),
    )(tokens, weight_codes, weight_scales, down, up, rows, adapter_slot, live_rows)


def solution(mesh):
    in_specs = (
        P(("req", "tp"), None),
        P("req", "tp"),
        P("req", "tp"),
        P("req", "tp", None),
        P("req", None, "tp"),
        P(),
        P(),
        P(),
    )
    return jax.shard_map(body, mesh=mesh, in_specs=in_specs, out_specs=P("req", "tp"), check_vma=False)
```
